512 devices in a mesh: tm: 16 (over y, x), feat: 32 (over z, core).
Axes of the slice: x: 4, y: 4, z: 16, core: 2. Of those that a mesh axis runs over, the one named last changes fastest.
Arguments:
- bin_index: int32 [1024, 16384], P('feat', 'tm'), may hold values from 0 to 255
- node_ids: int32 [16384], P('tm'), may hold values from 0 to 31
- logits: float32 [16384], P(('tm', 'feat')), may hold values from -8 to 8
- labels: int32 [16384], P(('tm', 'feat')), may hold values 0 or 1
- roots: int32 [16], replicated, may hold values from 1 to 32
Outputs:
- split_gain: float32 [16, 32, 1024], P(None, None, 'feat')
- node_gain: float32 [16, 32], replicated
The draws below stay inside these ranges and needn't reach their ends.
All inputs are finite; a program needn't handle non-finite values. No bound on the sum of `labels` on one device may be relied on, other than what follows from the above.
Results may differ from the reference program's by a relative error of at most 0.0021.
Values may be sent and summed in bfloat16 or wider, within the bound.
A program may use at most 128 MiB of HBM per device.

```python
import jax
import jax.numpy as jnp
from jax import lax

FEATURES = 1024
BINS = 256
NODES = 32
FOLDS = 16
BLOCKS_DEV = 2
BLOCK_ROWS = 512
TIME_BLOCKS = 32
ROWS = 16384
N_TM = 16


def place_ends(entries, stream_key, smallest, largest):
    dims = entries.shape
    spot = [jax.random.randint(jax.random.fold_in(stream_key, axis), (), 0, dims[axis]) for axis in range(len(dims))]
    entries = entries.at[tuple(spot)].set(smallest)
    longest = dims.index(max(dims))
    spot[longest] = (spot[longest] + 1) % dims[longest]
    return entries.at[tuple(spot)].set(largest)


def levels(key, extent, pieces, least, high):
    factor_of, own = 1.0, jax.random.fold_in(key, 6)
    for axis_at, shards_of in pieces:
        steps = jnp.exp(jax.random.uniform(jax.random.fold_in(own, axis_at), (shards_of,), jnp.float32, least / len(pieces), high / len(pieces)))
        factor_of = factor_of * jnp.repeat(steps, extent[axis_at] // shards_of).reshape([-1 if axis == axis_at else 1 for axis in range(len(extent))])
    return factor_of


def bell_draw(own_key, shape, scale, bound, pieces=(), kind=jnp.bfloat16):
    drawn = jax.random.normal(own_key, shape, jnp.float32) * scale
    if len(pieces) > 0:
        drawn = levels(own_key, shape, pieces, -0.22, 0.18) * drawn
    return jnp.clip(drawn, min=-bound, max=bound).astype(kind)


def setup_inputs(seed: int = 0) -> dict:
    streams_of = jax.random.split(jax.random.key(seed), 6)
    return {
        "bin_index": place_ends(jax.random.randint(streams_of[0], (FEATURES, ROWS), 0, BINS), jax.random.fold_in(streams_of[0], 1), 0, BINS - 1).astype(jnp.int32),
        "node_ids": place_ends(jax.random.randint(streams_of[1], (ROWS,), 0, NODES), jax.random.fold_in(streams_of[1], 1), 0, NODES - 1).astype(jnp.int32),
        "logits": bell_draw(streams_of[2], (ROWS,), 2.0, 8.0, ((0, 512),), jnp.float32),
        "labels": place_ends((jax.random.randint(streams_of[3], (ROWS,), 0, 2) < 1).astype(jnp.int32), jax.random.fold_in(streams_of[3], 1), 0, 1),
        "roots": place_ends(jax.random.randint(streams_of[4], (FOLDS,), 1, BLOCKS_DEV * N_TM + 1), jax.random.fold_in(streams_of[4], 1), 1, BLOCKS_DEV * N_TM).astype(jnp.int32),
    }


ridge = 1.0


def best_gain(grad_sum, hess_sum):
    left_grad = jnp.cumsum(grad_sum, axis=-1)
    left_hess = jnp.cumsum(hess_sum, axis=-1)
    total_grad = left_grad[..., -1:]
    total_hess = left_hess[..., -1:]
    left_grad = left_grad[..., :-1]
    left_hess = left_hess[..., :-1]
    right_grad = total_grad - left_grad
    right_hess = total_hess - left_hess
    gains = (left_grad * left_grad / (left_hess + ridge)
             + right_grad * right_grad / (right_hess + ridge)
             - total_grad * total_grad / (total_hess + ridge))
    return jnp.max(gains, axis=-1)


def reference(bin_index, node_ids, logits, labels, roots):
    probability = jax.nn.sigmoid(logits)
    gradient = (probability - labels.astype(jnp.float32)).astype(jnp.bfloat16)
    hessian = (probability * (1.0 - probability)).astype(jnp.bfloat16)
    gradient, hessian = lax.optimization_barrier((gradient, hessian))
    gradient = gradient.astype(jnp.float32)
    hessian = hessian.astype(jnp.float32)
    segments = NODES * FEATURES * BINS
    feature_ids = jnp.arange(FEATURES, dtype=jnp.int32)[:, None]

    def per_block(carry, block_at):
        offset = (block_at * BLOCK_ROWS).astype(jnp.int32)
        columns = lax.dynamic_slice_in_dim(bin_index, offset, BLOCK_ROWS, 1)
        block_nodes = lax.dynamic_slice_in_dim(node_ids, offset, BLOCK_ROWS, 0)
        block_grad = lax.dynamic_slice_in_dim(gradient, offset, BLOCK_ROWS, 0)
        block_hess = lax.dynamic_slice_in_dim(hessian, offset, BLOCK_ROWS, 0)
        flat_ids = ((block_nodes[None, :] * FEATURES + feature_ids) * BINS + columns).reshape(-1)
        grad_weights = jnp.broadcast_to(block_grad[None, :], columns.shape).reshape(-1)
        hess_weights = jnp.broadcast_to(block_hess[None, :], columns.shape).reshape(-1)
        grad_hist = carry[0] + jax.ops.segment_sum(grad_weights, flat_ids, num_segments=segments)
        hess_hist = carry[1] + jax.ops.segment_sum(hess_weights, flat_ids, num_segments=segments)
        shaped = best_gain(grad_hist.reshape(NODES, FEATURES, BINS), hess_hist.reshape(NODES, FEATURES, BINS))
        return (grad_hist, hess_hist), shaped

    initial = (jnp.zeros((segments,), jnp.float32), jnp.zeros((segments,), jnp.float32))
    final_state, boundary = lax.scan(per_block, initial, jnp.arange(TIME_BLOCKS, dtype=jnp.int32))
    split_gain = jnp.take(boundary, (roots - 1).astype(jnp.int32), axis=0)
    node_gain = jnp.max(split_gain, axis=2)
    return split_gain, node_gain
```

```python
import functools

import jax
import jax.numpy as jnp
from jax import lax
from jax.experimental import pallas as pl
from jax.experimental.pallas import tpu as pltpu
from jax.sharding import PartitionSpec as P

BINS = 256
NODES = 32
FOLDS = 16
LANES = 128
STEPS = 8
QUARTERS = 4
SUB = 4
MESH = pl.DeviceIdType.MESH
RIDGE = 1.0
F32 = jnp.float32
BF16 = jnp.bfloat16


def kernel(
    n_tm,
    n_feat,
    bins_ref,
    node_ref,
    logits_ref,
    labels_ref,
    roots_ref,
    split_ref,
    best_ref,
    send0,
    recv0,
    send1,
    recv1,
    send2,
    recv2,
    send4,
    recv4,
    send5,
    recv5,
    mask,
    sums,
    carry,
    gains,
    rolled,
    send_sems,
    recv_sems,
):
    tm = lax.axis_index("tm")
    feat = lax.axis_index("feat")

    def tm_peer(d):
        return lax.rem(tm + d, n_tm)

    def feat_peer(d):
        return lax.rem(feat + d, n_feat)

    barrier = pltpu.get_barrier_semaphore()
    for d in range(1, n_tm):
        pl.semaphore_signal(barrier, inc=1, device_id=(tm_peer(d), feat), device_id_type=MESH)
    for d in range(1, n_feat):
        pl.semaphore_signal(barrier, inc=1, device_id=(tm, feat_peer(d)), device_id_type=MESH)

    logits = jnp.concatenate([logits_ref[...]] * 4, axis=1)
    labels = jnp.concatenate([labels_ref[...]] * 4, axis=1).astype(F32)
    lane = lax.broadcasted_iota(jnp.int32, (1, LANES), 1)
    own = lane // 32 == lax.rem(feat, 4)
    prob = 1.0 / (1.0 + jnp.exp(-logits))
    grad = jnp.where(own, prob - labels, 0.0)
    hess = jnp.where(own, prob * (1.0 - prob), 0.0)
    send1[...] = jnp.concatenate([grad, hess], axis=0)

    nodes = node_ref[...].astype(F32)
    for t in range(n_tm):
        rows = []
        for f in (2 * t, 2 * t + 1):
            at = (f // 8) * 64 + f % 8
            rows.append(bins_ref[pl.ds(at, 8, stride=8), :].astype(F32))
        send0[t] = jnp.concatenate(rows + [nodes, nodes], axis=0).astype(BF16)

    pl.semaphore_wait(barrier, n_tm + n_feat - 2)

    def send(src, dst, phase, device):
        pltpu.make_async_remote_copy(
            src_ref=src,
            dst_ref=dst,
            send_sem=send_sems.at[phase],
            recv_sem=recv_sems.at[phase],
            device_id=device,
            device_id_type=MESH,
        ).start()

    def received(whole, phase):
        pltpu.make_async_copy(whole, whole, recv_sems.at[phase]).wait()

    def sent(part, phase):
        pltpu.make_async_copy(part, part, send_sems.at[phase]).wait()

    for d in range(1, n_feat):
        send(send1, recv1.at[feat], 1, (tm, feat_peer(d)))
    pltpu.make_async_copy(send1, recv1.at[feat], recv_sems.at[1]).start()
    for d in range(1, n_tm):
        send(send0.at[tm_peer(d)], recv0.at[tm], 0, (tm_peer(d), feat))
    pltpu.make_async_copy(send0.at[tm], recv0.at[tm], recv_sems.at[0]).start()

    received(recv1, 1)
    rows = []
    for s in range(8):
        rows.append((recv1[4 * s] + recv1[4 * s + 1]) + (recv1[4 * s + 2] + recv1[4 * s + 3]))
    send2[...] = jnp.concatenate(rows, axis=0).astype(BF16)

    for d in range(1, n_tm):
        send(send2, recv2.at[tm], 2, (tm_peer(d), feat))
    pltpu.make_async_copy(send2, recv2.at[tm], recv_sems.at[2]).start()

    received(recv0, 0)
    level = lax.broadcasted_iota(jnp.int32, (16, LANES), 0).astype(F32)
    one = jnp.ones((16, LANES), BF16)
    zero = jnp.zeros((16, LANES), BF16)

    def make_mask(i, _):
        half = lax.rem(i, 2)
        for j in range(QUARTERS):
            t = 4 * j + i // 2
            tile = recv0[t].astype(F32)
            for f in range(2):
                both = tile[8 * f : 8 * f + 8]
                four = jnp.where(half == 0, both[:4], both[4:])
                for s in range(SUB):
                    b16 = jnp.broadcast_to(four[s : s + 1], (16, LANES)).astype(BF16)
                    at = (j * SUB + s) * LANES
                    for v in range(BINS // 16):
                        cut = (level + 16.0 * v).astype(BF16)
                        mask[i, pl.ds(f * BINS + 16 * v, 16), pl.ds(at, LANES)] = jnp.where(
                            cut >= b16, one, zero
                        )
        return 0

    lax.fori_loop(0, STEPS, make_mask, 0)

    received(recv2, 2)
    node_level = lax.broadcasted_iota(jnp.int32, (NODES, LANES), 0).astype(F32)

    def accumulate(i, _):
        half = lax.rem(i, 2)
        quarters = []
        for j in range(QUARTERS):
            t = 4 * j + i // 2
            gh = recv2[t].astype(F32)
            gh = jnp.where(half == 0, gh[:8], gh[8:])
            node = recv0[t].astype(F32)[16:24]
            node = jnp.where(half == 0, node[:4], node[4:])
            grads, hesss = [], []
            for s in range(SUB):
                here = jnp.broadcast_to(node[s : s + 1], (NODES, LANES)) == node_level
                grads.append(jnp.where(here, jnp.broadcast_to(gh[2 * s : 2 * s + 1], (NODES, LANES)), 0.0).astype(BF16))
                hesss.append(jnp.where(here, jnp.broadcast_to(gh[2 * s + 1 : 2 * s + 2], (NODES, LANES)), 0.0).astype(BF16))
            grads = jnp.concatenate(grads, axis=1)
            hesss = jnp.concatenate(hesss, axis=1)
            pieces = []
            for kind in (grads, hesss):
                for q in range(QUARTERS):
                    pieces.append(kind if q == j else jnp.zeros_like(kind))
            quarters.append(jnp.concatenate(pieces, axis=0))
        weights = jnp.concatenate(quarters, axis=1)
        new = lax.dot_general(
            mask[i], weights, (((1,), (1,)), ((), ())), preferred_element_type=F32
        )

        @pl.when(i == 0)
        def _():
            sums[0] = new

        @pl.when(i > 0)
        def _():
            sums[i] = sums[jnp.maximum(i - 1, 0)] + new

        return 0

    lax.fori_loop(0, STEPS, accumulate, 0)

    wide = lax.broadcasted_iota(jnp.int32, (64, LANES), 1)

    def make_carry(c, _):
        at = pl.ds(pl.multiple_of(c * 64, 64), 64)
        for kind in range(2):
            cols = pl.ds(kind * LANES, LANES)
            total = sums[STEPS - 1, at, cols]
            shifted = jnp.where(wide >= 32, pltpu.roll(total, 32, 1), 0.0)
            acc = shifted + jnp.where(wide >= 64, pltpu.roll(total, 64, 1), 0.0)
            carry[at, cols] = acc + jnp.where(wide >= 96, pltpu.roll(total, 96, 1), 0.0)
        return 0

    lax.fori_loop(0, 8, make_carry, 0)

    chunk = 32
    last = lax.broadcasted_iota(jnp.int32, (chunk, LANES), 0) == chunk - 1

    def make_gains(i, _):
        for f in range(2):
            top = f * BINS + BINS - 1
            g_cols, h_cols = pl.ds(0, LANES), pl.ds(LANES, LANES)
            end = pl.ds(top, 1)
            g_all = sums[i, end, g_cols] + carry[end, g_cols]
            h_all = sums[i, end, h_cols] + carry[end, h_cols]
            best = None
            for c in range(BINS // chunk):
                at = pl.ds(f * BINS + c * chunk, chunk)
                g_left = sums[i, at, g_cols] + carry[at, g_cols]
                h_left = sums[i, at, h_cols] + carry[at, h_cols]
                g_right = g_all - g_left
                h_right = (h_all - h_left) + RIDGE
                h_left = h_left + RIDGE
                gain = (g_left * g_left * h_right + g_right * g_right * h_left) / (h_left * h_right)
                if c == BINS // chunk - 1:
                    gain = jnp.where(last, -jnp.inf, gain)
                best = gain if best is None else jnp.maximum(best, gain)
            best = jnp.max(best, axis=0, keepdims=True)
            gains[pl.ds(f * STEPS + i, 1), :] = best - g_all * g_all / (h_all + RIDGE)
        return 0

    lax.fori_loop(0, STEPS, make_gains, 0)

    for f in range(2):
        rows = gains[pl.ds(f * STEPS, STEPS), :]
        for r in range(QUARTERS):
            rolled[pl.ds(f * 32 + r * STEPS, STEPS), :] = rows if r == 0 else pltpu.roll(rows, 32 * r, 1)
    packed = []
    for f in range(2):
        for a in range(4):
            row = None
            for q in range(4):
                block = roots_ref[4 * q + a] - 1
                j = block // STEPS
                i = block - j * STEPS
                r = lax.rem(q - j + QUARTERS, QUARTERS)
                picked = rolled[pl.ds(f * 32 + r * STEPS + i, 1), :]
                row = picked if row is None else jnp.where(lane >= 32 * q, picked, row)
            packed.append(row)
    send4[...] = jnp.concatenate(packed, axis=0)

    mine = pl.ds(pl.multiple_of(tm * 8, 8), 8)
    for d in range(1, n_tm):
        send(send4, recv4.at[mine], 3, (tm_peer(d), feat))
    pltpu.make_async_copy(send4, recv4.at[mine], recv_sems.at[3]).start()
    received(recv4, 3)

    top = recv4[pl.ds(0, 8), :]
    for t in range(1, n_tm):
        top = jnp.maximum(top, recv4[pl.ds(8 * t, 8), :])
    send5[...] = jnp.maximum(top[:4], top[4:])
    for d in range(1, n_feat):
        send(send5, recv5.at[feat], 4, (tm, feat_peer(d)))
    pltpu.make_async_copy(send5, recv5.at[feat], recv_sems.at[4]).start()

    for a in range(4):
        turned = jnp.transpose(recv4[pl.ds(a, 2 * n_tm, stride=4), :])
        for q in range(4):
            split_ref[4 * q + a] = turned[32 * q : 32 * q + 32]

    sent(recv0.at[pl.ds(0, n_tm - 1)], 0)
    sent(recv1.at[pl.ds(0, n_feat - 1)], 1)
    sent(recv2.at[pl.ds(0, n_tm - 1)], 2)
    sent(recv4.at[pl.ds(0, 8 * (n_tm - 1))], 3)
    received(recv5, 4)
    top = recv5[0]
    for f in range(1, n_feat):
        top = jnp.maximum(top, recv5[f])
    for q in range(4):
        best_ref[pl.ds(4 * q, 4), :] = top[:, 32 * q : 32 * q + 32]
    sent(recv5.at[pl.ds(0, n_feat - 1)], 4)


def local(n_tm, n_feat, bin_index, node_ids, logits, labels, roots):
    bins = bin_index.reshape(4, 8, 8, LANES).transpose(0, 2, 1, 3).reshape(256, LANES)
    vmem = pl.BlockSpec(memory_space=pltpu.VMEM)
    smem = pl.BlockSpec(memory_space=pltpu.SMEM)
    return pl.pallas_call(
        functools.partial(kernel, n_tm, n_feat),
        out_shape=(
            jax.ShapeDtypeStruct((FOLDS, NODES, 2 * n_tm), F32),
            jax.ShapeDtypeStruct((FOLDS, NODES), F32),
        ),
        in_specs=[vmem, vmem, vmem, vmem, smem],
        out_specs=(vmem, vmem),
        scratch_shapes=[
            pltpu.VMEM((n_tm, 32, LANES), BF16),
            pltpu.VMEM((n_tm, 32, LANES), BF16),
            pltpu.VMEM((2, LANES), F32),
            pltpu.VMEM((n_feat, 2, LANES), F32),
            pltpu.VMEM((16, LANES), BF16),
            pltpu.VMEM((n_tm, 16, LANES), BF16),
            pltpu.VMEM((8, LANES), F32),
            pltpu.VMEM((8 * n_tm, LANES), F32),
            pltpu.VMEM((4, LANES), F32),
            pltpu.VMEM((n_feat, 4, LANES), F32),
            pltpu.VMEM((STEPS, 2 * BINS, QUARTERS * SUB * LANES), BF16),
            pltpu.VMEM((STEPS, 2 * BINS, 2 * LANES), F32),
            pltpu.VMEM((2 * BINS, 2 * LANES), F32),
            pltpu.VMEM((2 * STEPS, LANES), F32),
            pltpu.VMEM((2 * QUARTERS * STEPS, LANES), F32),
            pltpu.SemaphoreType.DMA((5,)),
            pltpu.SemaphoreType.DMA((5,)),
        ],
        compiler_params=pltpu.CompilerParams(
            collective_id=0, has_side_effects=True, vmem_limit_bytes=48 * 1024 * 1024
        ),
    )(bins, node_ids.reshape(8, LANES), logits.reshape(1, 32), labels.reshape(1, 32), roots)


def solution(mesh):
    in_specs = (P("feat", "tm"), P("tm"), P(("tm", "feat")), P(("tm", "feat")), P())
    out_specs = (P(None, None, "feat"), P())
    body = functools.partial(local, mesh.shape["tm"], mesh.shape["feat"])
    return jax.shard_map(body, mesh=mesh, in_specs=in_specs, out_specs=out_specs, check_vma=False)
```

```python
import functools

import jax
import jax.numpy as jnp
from jax import lax
from jax.experimental import pallas as pl
from jax.experimental.pallas import tpu as pltpu
from jax.sharding import PartitionSpec as P

BINS = 256
NODES = 32
FOLDS = 16
LANES = 128
STEPS = 8
QUARTERS = 4
SUBS = 8
MESH = pl.DeviceIdType.MESH
RIDGE = 1.0
UNROLL = 6
F32 = jnp.float32
BF16 = jnp.bfloat16


def kernel(
    n_tm,
    n_z,
    bins_hbm,
    node_hbm,
    logits_hbm,
    labels_hbm,
    roots_hbm,
    split_ref,
    best_ref,
    bins_ref,
    node_ref,
    logits_ref,
    labels_ref,
    roots_ref,
    fold_row,
    send0,
    recv0,
    send1,
    recv1,
    send2,
    recv2,
    send4,
    recv4,
    top4,
    recv_top,
    send5,
    recv5,
    mask,
    node_rows,
    sums,
    slope,
    total,
    grad_end,
    hess_end,
    gains,
    rolled,
    load_sems,
    send_sems,
    recv_sems,
    pair_sems,
    reach,
):
    tm = lax.axis_index("tm")
    feat = lax.axis_index("feat")
    z = feat // 2
    core = lax.rem(feat, 2)

    def tm_peer(d):
        return (lax.rem(tm + d, n_tm), feat)

    def tm_other(d):
        return (lax.rem(tm + d, n_tm), feat + 1 - 2 * core)

    def z_peer(d):
        return (tm, 2 * lax.rem(z + d, n_z) + core)

    z_order = sorted(range(1, n_z), key=lambda d: -min(d, n_z - d))
    near = n_z // 4
    peers = [tm_peer(d) for d in range(1, n_tm)] + [tm_other(d) for d in range(n_tm)]
    peers += [z_peer(d) for d in z_order if min(d, n_z - d) <= near]

    barrier = pltpu.get_barrier_semaphore()
    for peer in peers:
        pl.semaphore_signal(barrier, inc=1, device_id=peer, device_id_type=MESH)

    loads = [
        pltpu.make_async_copy(src, dst, load_sems.at[k])
        for k, (src, dst) in enumerate(
            [
                (logits_hbm, logits_ref),
                (labels_hbm, labels_ref),
                (bins_hbm, bins_ref),
                (node_hbm, node_ref),
                (roots_hbm, roots_ref),
            ]
        )
    ]
    for load in loads:
        load.start()

    loads[0].wait()
    loads[1].wait()
    logits = jnp.concatenate([logits_ref[...]] * 4, axis=1)
    labels = jnp.concatenate([labels_ref[...]] * 4, axis=1).astype(F32)
    lane = lax.broadcasted_iota(jnp.int32, (1, LANES), 1)
    place = core + 2 * lax.rem(z, 2)
    prob = 1.0 / (1.0 + jnp.exp(-logits))
    send1[...] = jnp.where(lane // 32 == place, prob - labels, 0.0) + jnp.where(
        lane // 32 == lax.rem(place + 2, 4), prob * (1.0 - prob), 0.0
    )

    loads[2].wait()
    loads[3].wait()
    nodes = node_ref[...].astype(F32)
    for t in range(n_tm):
        rows = []
        for f in (2 * t, 2 * t + 1):
            at = (f // 8) * 64 + f % 8
            rows.append(bins_ref[pl.ds(at, 8, stride=8), :].astype(F32))
        send0[t] = jnp.concatenate(rows + [nodes, nodes], axis=0).astype(BF16)

    pl.semaphore_wait(barrier, len(peers))
    pl.semaphore_signal(reach, inc=1, device_id=z_peer(near), device_id_type=MESH)
    pl.semaphore_signal(reach, inc=1, device_id=z_peer(n_z - near), device_id_type=MESH)

    def send(src, dst, send_sem, recv_sem, device):
        pltpu.make_async_remote_copy(
            src_ref=src,
            dst_ref=dst,
            send_sem=send_sem,
            recv_sem=recv_sem,
            device_id=device,
            device_id_type=MESH,
        ).start()

    def largest(rows):
        while len(rows) > 1:
            rest = rows[len(rows) // 2 * 2 :]
            rows = [jnp.maximum(a, b) for a, b in zip(rows[::2], rows[1::2])] + rest
        return rows[0]

    def wait(whole, sem):
        pltpu.make_async_copy(whole, whole, sem).wait()

    row = recv1.at[core * n_tm + tm]
    for d in range(1, n_tm):
        send(send1, row, send_sems.at[1], recv_sems.at[1], tm_peer(d))
    for d in range(n_tm):
        send(send1, row, send_sems.at[1], recv_sems.at[1], tm_other(d))
    pltpu.make_async_copy(send1, row, recv_sems.at[1]).start()
    for d in range(1, n_tm):
        device = tm_peer(d)
        send(send0.at[device[0]], recv0.at[tm], send_sems.at[0], recv_sems.at[0], device)
    pltpu.make_async_copy(send0.at[tm], recv0.at[tm], recv_sems.at[0]).start()

    def clear(i, _):
        sums[i] = jnp.zeros((2 * BINS, 2 * LANES), F32)
        return 0

    lax.fori_loop(0, STEPS, clear, 0)

    loads[4].wait()
    for o in range(FOLDS):
        block = roots_ref[o] - 1
        fold_row[o] = (((o // 4 - (block >> 3)) & 3) << 3) + (block & 7)

    wait(recv1, recv_sems.at[1])
    send2[...] = jnp.concatenate([recv1[t] + recv1[n_tm + t] for t in range(n_tm)], axis=0).astype(BF16)

    pl.semaphore_wait(reach, 2)
    for d in z_order:
        send(send2, recv2.at[z], send_sems.at[2], pair_sems.at[z // 2], z_peer(d))
    pltpu.make_async_copy(send2, recv2.at[z], pair_sems.at[z // 2]).start()

    wait(recv0, recv_sems.at[0])
    level = lax.broadcasted_iota(jnp.int32, (16, LANES), 0).astype(F32)
    one = jnp.ones((16, LANES), BF16)
    zero = jnp.zeros((16, LANES), BF16)

    def make_mask(tt, _):
        for j in range(QUARTERS):
            tile = recv0[4 * j + tt].astype(F32)
            for s in range(SUBS):
                node_rows[s, tt, pl.ds(j, 1), :] = tile[16 + s : 17 + s]
                for f in range(2):
                    b16 = jnp.broadcast_to(tile[8 * f + s : 8 * f + s + 1], (16, LANES)).astype(BF16)
                    for v in range(BINS // 16):
                        cut = (level + 16.0 * v).astype(BF16)
                        mask[s, tt, pl.ds(f * BINS + 16 * v, 16), pl.ds(j * LANES, LANES)] = jnp.where(
                            cut >= b16, one, zero
                        )
        return 0

    lax.fori_loop(0, 4, make_mask, 0)

    node_level = lax.broadcasted_iota(jnp.int32, (NODES, LANES), 0).astype(F32)
    low = lax.broadcasted_iota(jnp.int32, (16, LANES), 1) < 64
    blank = jnp.zeros((NODES, LANES), BF16)

    def accumulate(o, odd):
        near = (o + 1) // 2
        s = lax.rem(z // 2 + (near if odd else SUBS - near), SUBS)
        wait(recv2.at[pl.ds(2 * s, 2)], pair_sems.at[s])
        first = recv2[2 * s].astype(F32)
        second = recv2[2 * s + 1].astype(F32)
        grads = jnp.where(low, first, second)
        hesss = pltpu.roll(jnp.where(low, second, first), 64, 1)
        for tt in range(4):
            node = node_rows[s, tt]
            quarters = []
            for j in range(QUARTERS):
                t = 4 * j + tt
                here = jnp.broadcast_to(node[j : j + 1], (NODES, LANES)) == node_level
                pieces = []
                for kind in (grads, hesss):
                    chosen = jnp.where(here, jnp.broadcast_to(kind[t : t + 1], (NODES, LANES)), 0.0).astype(BF16)
                    pieces += [chosen if q == j else blank for q in range(QUARTERS)]
                quarters.append(jnp.concatenate(pieces, axis=0))
            weights = jnp.concatenate(quarters, axis=1)
            sums[2 * tt + s // 4] += lax.dot_general(
                mask[s, tt], weights, (((1,), (1,)), ((), ())), preferred_element_type=F32
            )
        return 0

    def accumulate_two(o, _):
        accumulate(2 * o, False)
        accumulate(2 * o + 1, True)
        return 0

    lax.fori_loop(0, SUBS // 2 - 1, accumulate_two, 0)
    accumulate(SUBS - 2, False)
    accumulate(SUBS - 1, True)

    lane8 = lax.broadcasted_iota(jnp.int32, (8, LANES), 1)
    kinds = (pl.ds(0, LANES), pl.ds(LANES, LANES))

    def prefixes(at):
        out = []
        for cols, ridge in zip(kinds, (0.0, RIDGE)):
            run = [sums[0, at, cols]]
            for i in range(1, STEPS):
                run.append(run[-1] + sums[i, at, cols])
            before = jnp.where(lane8 >= 32, pltpu.roll(run[-1], 32, 1), 0.0) + ridge
            before = before + jnp.where(lane8 >= 64, pltpu.roll(run[-1], 64, 1), 0.0)
            before = before + jnp.where(lane8 >= 96, pltpu.roll(run[-1], 96, 1), 0.0)
            out.append([r + before for r in run])
        return out

    last_row = lax.broadcasted_iota(jnp.int32, (8, LANES), 0) == 7
    for f in range(2):
        end = pl.ds(f * BINS + BINS - 8, 8)
        grads, hesss = prefixes(end)
        for i in range(STEPS):
            g_all = jnp.broadcast_to(grads[i][7:8], (8, LANES))
            s_all = jnp.broadcast_to(hesss[i][7:8], (8, LANES)) + RIDGE
            slope[i] = g_all / s_all
            total[i] = s_all
            grad_end[pl.ds(i, 1), :] = grads[i][7:8]
            hess_end[pl.ds(i, 1), :] = hesss[i][7:8]

        def chunk(at, drop):
            grads, hesss = prefixes(at)
            out = []
            for i in range(STEPS):
                a = hesss[i]
                apart = grads[i] - a * slope[i]
                product = a * (total[i] - a)
                inverse = pl.reciprocal(product, approx=True)
                inverse = inverse * (2.0 - product * inverse)
                gain = apart * apart * inverse
                out.append(jnp.where(last_row, 0.0, gain) if drop else gain)
            return out

        def scan(c, best):
            for k in range(UNROLL):
                at = pl.ds(pl.multiple_of(f * BINS + 8 * (UNROLL * c + k), 8), 8)
                best = [jnp.maximum(b, g) for b, g in zip(best, chunk(at, False))]
            return tuple(best)

        best = tuple(chunk(end, True))
        rounds = (BINS // 8 - 1) // UNROLL
        best = lax.fori_loop(0, rounds, scan, best)
        for c in range(rounds * UNROLL, BINS // 8 - 1):
            best = [jnp.maximum(b, g) for b, g in zip(best, chunk(pl.ds(f * BINS + 8 * c, 8), False))]
        best = jnp.concatenate([jnp.max(b, axis=0, keepdims=True) for b in best], axis=0)
        s_less = hess_end[...]
        g_all = grad_end[...]
        s_all = s_less + RIDGE
        gains[pl.ds(f * STEPS, STEPS), :] = s_all * best - g_all * g_all / (s_all * s_less)

    for f in range(2):
        rows = gains[pl.ds(f * STEPS, STEPS), :]
        for r in range(QUARTERS):
            rolled[pl.ds(f * 32 + r * STEPS, STEPS), :] = rows if r == 0 else pltpu.roll(rows, 32 * r, 1)
    packed = []
    for f in range(2):
        for a in range(4):
            row = None
            for q in range(4):
                picked = rolled[pl.ds(f * 32 + fold_row[4 * q + a], 1), :]
                row = picked if row is None else jnp.where(lane >= 32 * q, picked, row)
            packed.append(row)
    packed = jnp.concatenate(packed, axis=0)
    send4[...] = packed
    top4[...] = jnp.maximum(packed[:4], packed[4:])

    mine = pl.ds(pl.multiple_of(tm * 8, 8), 8)
    for d in range(1, n_tm):
        send(send4, recv4.at[mine], send_sems.at[3], recv_sems.at[3], tm_peer(d))
    for d in range(n_tm):
        send(top4, recv_top.at[tm], send_sems.at[4], recv_sems.at[4], tm_other(d))
    pltpu.make_async_copy(send4, recv4.at[mine], recv_sems.at[3]).start()
    wait(recv4, recv_sems.at[3])
    wait(recv_top, recv_sems.at[4])

    top = largest([recv4[pl.ds(8 * t, 8), :] for t in range(n_tm)])
    send5[...] = largest([top[:4], top[4:]] + [recv_top[t] for t in range(n_tm)])
    for d in z_order:
        send(send5, recv5.at[z], send_sems.at[5], recv_sems.at[5], z_peer(d))
    pltpu.make_async_copy(send5, recv5.at[z], recv_sems.at[5]).start()

    for a in range(4):
        turned = jnp.transpose(recv4[pl.ds(a, 2 * n_tm, stride=4), :])
        for q in range(4):
            split_ref[4 * q + a] = turned[32 * q : 32 * q + 32]

    wait(recv0.at[pl.ds(0, n_tm - 1)], send_sems.at[0])
    wait(recv1.at[pl.ds(0, 2 * n_tm - 1)], send_sems.at[1])
    wait(recv2.at[pl.ds(0, n_z - 1)], send_sems.at[2])
    wait(recv4.at[pl.ds(0, 8 * (n_tm - 1))], send_sems.at[3])
    wait(recv_top, send_sems.at[4])
    wait(recv5, recv_sems.at[5])
    top = largest([recv5[k] for k in range(n_z)])
    for q in range(4):
        best_ref[pl.ds(4 * q, 4), :] = top[:, 32 * q : 32 * q + 32]
    wait(recv5.at[pl.ds(0, n_z - 1)], send_sems.at[5])


def local(n_tm, n_feat, bin_index, node_ids, logits, labels, roots):
    n_z = n_feat // 2
    bins = bin_index.reshape(4, 8, 8, LANES).transpose(0, 2, 1, 3).reshape(256, LANES)
    operands = (bins, node_ids.reshape(8, LANES), logits.reshape(1, 32), labels.reshape(1, 32), roots)
    vmem = pl.BlockSpec(memory_space=pltpu.VMEM)
    hbm = pl.BlockSpec(memory_space=pltpu.HBM)
    return pl.pallas_call(
        functools.partial(kernel, n_tm, n_z),
        out_shape=(
            jax.ShapeDtypeStruct((FOLDS, NODES, 2 * n_tm), F32),
            jax.ShapeDtypeStruct((FOLDS, NODES), F32),
        ),
        in_specs=[hbm] * 5,
        out_specs=(vmem, vmem),
        scratch_shapes=[
            pltpu.VMEM((256, LANES), jnp.int32),
            pltpu.VMEM((8, LANES), jnp.int32),
            pltpu.VMEM((1, 32), F32),
            pltpu.VMEM((1, 32), jnp.int32),
            pltpu.SMEM((FOLDS,), jnp.int32),
            pltpu.SMEM((FOLDS,), jnp.int32),
            pltpu.VMEM((n_tm, 32, LANES), BF16),
            pltpu.VMEM((n_tm, 32, LANES), BF16),
            pltpu.VMEM((1, LANES), F32),
            pltpu.VMEM((2 * n_tm, 1, LANES), F32),
            pltpu.VMEM((n_tm, LANES), BF16),
            pltpu.VMEM((n_z, n_tm, LANES), BF16),
            pltpu.VMEM((8, LANES), F32),
            pltpu.VMEM((8 * n_tm, LANES), F32),
            pltpu.VMEM((4, LANES), F32),
            pltpu.VMEM((n_tm, 4, LANES), F32),
            pltpu.VMEM((4, LANES), F32),
            pltpu.VMEM((n_z, 4, LANES), F32),
            pltpu.VMEM((SUBS, 4, 2 * BINS, QUARTERS * LANES), BF16),
            pltpu.VMEM((SUBS, 4, QUARTERS, LANES), F32),
            pltpu.VMEM((STEPS, 2 * BINS, 2 * LANES), F32),
            pltpu.VMEM((STEPS, 8, LANES), F32),
            pltpu.VMEM((STEPS, 8, LANES), F32),
            pltpu.VMEM((STEPS, LANES), F32),
            pltpu.VMEM((STEPS, LANES), F32),
            pltpu.VMEM((2 * STEPS, LANES), F32),
            pltpu.VMEM((2 * QUARTERS * STEPS, LANES), F32),
            pltpu.SemaphoreType.DMA((5,)),
            pltpu.SemaphoreType.DMA((6,)),
            pltpu.SemaphoreType.DMA((6,)),
            pltpu.SemaphoreType.DMA((SUBS,)),
            pltpu.SemaphoreType.REGULAR,
        ],
        compiler_params=pltpu.CompilerParams(
            collective_id=0, has_side_effects=True, vmem_limit_bytes=32 * 1024 * 1024
        ),
    )(*[pltpu.with_memory_space_constraint(x, pltpu.HBM) for x in operands])


def solution(mesh):
    in_specs = (P("feat", "tm"), P("tm"), P(("tm", "feat")), P(("tm", "feat")), P())
    out_specs = (P(None, None, "feat"), P())
    body = functools.partial(local, mesh.shape["tm"], mesh.shape["feat"])
    return jax.shard_map(body, mesh=mesh, in_specs=in_specs, out_specs=out_specs, check_vma=False)
```

```python
import functools

import jax
import jax.numpy as jnp
from jax import lax
from jax.experimental import pallas as pl
from jax.experimental.pallas import tpu as pltpu
from jax.sharding import PartitionSpec as P

BINS = 256
NODES = 32
FOLDS = 16
LANES = 128
STEPS = 8
QUARTERS = 4
SUBS = 8
MESH = pl.DeviceIdType.MESH
RIDGE = 1.0
PAIR_ORDER = (
    (0, 1, 2, 3, 7, 6, 5, 4),
    (1, 0, 2, 3, 7, 6, 4, 5),
    (2, 1, 3, 0, 4, 7, 5, 6),
    (3, 2, 1, 0, 4, 5, 6, 7),
    (4, 3, 5, 2, 6, 1, 0, 7),
    (5, 4, 6, 3, 7, 2, 0, 1),
    (6, 7, 5, 0, 4, 1, 3, 2),
    (7, 0, 6, 1, 5, 2, 3, 4),
)
UNROLL = 8
F32 = jnp.float32
BF16 = jnp.bfloat16


def largest(rows):
    while len(rows) > 1:
        rest = rows[len(rows) // 2 * 2 :]
        rows = [jnp.maximum(a, b) for a, b in zip(rows[::2], rows[1::2])] + rest
    return rows[0]


def finish(split_ref, planes_ref, split_out, best_out, best_ref, sems):
    copy = pltpu.make_async_copy(split_ref, split_out, sems.at[0])
    copy.start()
    top = largest([planes_ref[k] for k in range(planes_ref.shape[0])])
    for q in range(4):
        best_ref[pl.ds(4 * q, 4), :] = top[:, 32 * q : 32 * q + 32]
    best_copy = pltpu.make_async_copy(best_ref, best_out, sems.at[1])
    best_copy.start()
    copy.wait()
    best_copy.wait()


def kernel(
    n_tm,
    n_z,
    bins_hbm,
    node_hbm,
    logits_hbm,
    labels_hbm,
    roots_hbm,
    split_ref,
    planes_ref,
    bins_ref,
    node_ref,
    logits_ref,
    labels_ref,
    roots_ref,
    fold_row,
    send0,
    recv0,
    send1,
    recv1,
    send2,
    recv2,
    send4,
    recv4,
    top4,
    recv_top,
    send5,
    recv5,
    mask,
    node_rows,
    sums,
    slope,
    total,
    grad_end,
    hess_end,
    gains,
    rolled,
    load_sems,
    send_sems,
    recv_sems,
    pair_sems,
    reach,
):
    tm = lax.axis_index("tm")
    feat = lax.axis_index("feat")
    z = feat // 2
    core = lax.rem(feat, 2)

    def tm_peer(d):
        return (lax.rem(tm + d, n_tm), feat)

    def tm_other(d):
        return (lax.rem(tm + d, n_tm), feat + 1 - 2 * core)

    def z_peer(d):
        return (tm, 2 * lax.rem(z + d, n_z) + core)

    def away(d):
        return min(d // 4, 4 - d // 4) + min(d % 4, 4 - d % 4)

    tm_order = sorted(range(n_tm), key=lambda d: -away(d))
    z_order = sorted(range(1, n_z), key=lambda d: -min(d, n_z - d))
    near = n_z // 4
    peers = [tm_other(d) for d in tm_order] + [tm_peer(d) for d in tm_order[:-1]]
    peers += [z_peer(d) for d in z_order if min(d, n_z - d) <= near]

    barrier = pltpu.get_barrier_semaphore()
    for peer in peers:
        pl.semaphore_signal(barrier, inc=1, device_id=peer, device_id_type=MESH)

    loads = [
        pltpu.make_async_copy(src, dst, load_sems.at[k])
        for k, (src, dst) in enumerate(
            [
                (logits_hbm, logits_ref),
                (labels_hbm, labels_ref),
                (bins_hbm, bins_ref),
                (node_hbm, node_ref),
                (roots_hbm, roots_ref),
            ]
        )
    ]
    for load in loads:
        load.start()

    loads[0].wait()
    loads[1].wait()
    logits = jnp.concatenate([logits_ref[...]] * 4, axis=1)
    labels = jnp.concatenate([labels_ref[...]] * 4, axis=1).astype(F32)
    lane = lax.broadcasted_iota(jnp.int32, (1, LANES), 1)
    place = core + 2 * lax.rem(z, 2)
    prob = 1.0 / (1.0 + jnp.exp(-logits))
    send1[...] = jnp.where(lane // 32 == place, prob - labels, 0.0) + jnp.where(
        lane // 32 == lax.rem(place + 2, 4), prob * (1.0 - prob), 0.0
    )

    loads[2].wait()
    loads[3].wait()
    nodes = node_ref[...].astype(F32)
    for t in range(n_tm):
        rows = []
        for f in (2 * t, 2 * t + 1):
            at = (f // 8) * 64 + f % 8
            rows.append(bins_ref[pl.ds(at, 8, stride=8), :].astype(F32))
        send0[t] = jnp.concatenate(rows + [nodes, nodes], axis=0).astype(BF16)

    pl.semaphore_wait(barrier, len(peers))
    pl.semaphore_signal(reach, inc=1, device_id=z_peer(near), device_id_type=MESH)
    pl.semaphore_signal(reach, inc=1, device_id=z_peer(n_z - near), device_id_type=MESH)

    def send(src, dst, send_sem, recv_sem, device):
        pltpu.make_async_remote_copy(
            src_ref=src,
            dst_ref=dst,
            send_sem=send_sem,
            recv_sem=recv_sem,
            device_id=device,
            device_id_type=MESH,
        ).start()

    def wait(whole, sem):
        pltpu.make_async_copy(whole, whole, sem).wait()

    row = recv1.at[core * n_tm + tm]
    for d in tm_order:
        send(send1, row, send_sems.at[1], recv_sems.at[1], tm_other(d))
        if d > 0:
            send(send1, row, send_sems.at[1], recv_sems.at[1], tm_peer(d))
    pltpu.make_async_copy(send1, row, recv_sems.at[1]).start()
    for d in tm_order[:-1]:
        device = tm_peer(d)
        send(send0.at[device[0]], recv0.at[tm], send_sems.at[0], recv_sems.at[0], device)
    pltpu.make_async_copy(send0.at[tm], recv0.at[tm], recv_sems.at[0]).start()

    def clear(i, _):
        sums[i] = jnp.zeros((2 * BINS, 2 * LANES), F32)
        return 0

    lax.fori_loop(0, STEPS, clear, 0)

    loads[4].wait()
    for o in range(FOLDS):
        block = roots_ref[o] - 1
        fold_row[o] = (((o // 4 - (block >> 3)) & 3) << 3) + (block & 7)

    wait(recv1, recv_sems.at[1])
    send2[...] = jnp.concatenate([recv1[t] + recv1[n_tm + t] for t in range(n_tm)], axis=0).astype(BF16)

    pl.semaphore_wait(reach, 2)
    for d in z_order[::-1]:
        send(send2, recv2.at[z], send_sems.at[2], pair_sems.at[z // 2], z_peer(d))
    pltpu.make_async_copy(send2, recv2.at[z], pair_sems.at[z // 2]).start()

    wait(recv0, recv_sems.at[0])
    level = lax.broadcasted_iota(jnp.int32, (16, LANES), 0).astype(F32)
    one = jnp.ones((16, LANES), BF16)
    zero = jnp.zeros((16, LANES), BF16)

    def make_mask(t, _):
        j, tt = t // 4, lax.rem(t, 4)
        tile = recv0[t].astype(F32)
        at = pl.multiple_of(j * LANES, LANES)
        for s in range(SUBS):
            node_rows[s, tt, pl.ds(j, 1), :] = tile[16 + s : 17 + s]
            for f in range(2):
                b16 = jnp.broadcast_to(tile[8 * f + s : 8 * f + s + 1], (16, LANES)).astype(BF16)
                for v in range(BINS // 16):
                    cut = (level + 16.0 * v).astype(BF16)
                    mask[s, tt, pl.ds(f * BINS + 16 * v, 16), pl.ds(at, LANES)] = jnp.where(cut >= b16, one, zero)
        return 0

    lax.fori_loop(0, n_tm, make_mask, 0)

    node_level = lax.broadcasted_iota(jnp.int32, (NODES, LANES), 0).astype(F32)
    low = lax.broadcasted_iota(jnp.int32, (16, LANES), 1) < 64
    blank = jnp.zeros((NODES, LANES), BF16)

    order = 0
    for pair_at, row in enumerate(PAIR_ORDER):
        code = sum(p << 3 * o for o, p in enumerate(row))
        order = jnp.where(z // 2 == pair_at, code, order)

    def pair(o):
        s = (order >> 3 * o) & 7
        wait(recv2.at[pl.ds(2 * s, 2)], pair_sems.at[s])
        return s

    def accumulate(s):
        first = recv2[2 * s].astype(F32)
        second = recv2[2 * s + 1].astype(F32)
        grads = jnp.where(low, first, second)
        hesss = pltpu.roll(jnp.where(low, second, first), 64, 1)
        for tt in range(4):
            node = node_rows[s, tt]
            quarters = []
            for j in range(QUARTERS):
                t = 4 * j + tt
                here = jnp.broadcast_to(node[j : j + 1], (NODES, LANES)) == node_level
                pieces = []
                for kind in (grads, hesss):
                    chosen = jnp.where(here, jnp.broadcast_to(kind[t : t + 1], (NODES, LANES)), 0.0).astype(BF16)
                    pieces += [chosen if q == j else blank for q in range(QUARTERS)]
                quarters.append(jnp.concatenate(pieces, axis=0))
            weights = jnp.concatenate(quarters, axis=1)
            sums[2 * tt + s // 4] += lax.dot_general(
                mask[s, tt], weights, (((1,), (1,)), ((), ())), preferred_element_type=F32
            )

    def accumulate_two(o, _):
        left, right = pair(2 * o), pair(2 * o + 1)
        accumulate(left)
        accumulate(right)
        return 0

    lax.fori_loop(0, SUBS // 2, accumulate_two, 0)

    lane8 = lax.broadcasted_iota(jnp.int32, (8, LANES), 1)
    kinds = (pl.ds(0, LANES), pl.ds(LANES, LANES))

    def prefixes(at):
        out = []
        for cols, ridge in zip(kinds, (0.0, RIDGE)):
            run = [sums[0, at, cols]]
            for i in range(1, STEPS):
                run.append(run[-1] + sums[i, at, cols])
            before = jnp.where(lane8 >= 32, pltpu.roll(run[-1], 32, 1), 0.0) + ridge
            before = before + jnp.where(lane8 >= 64, pltpu.roll(run[-1], 64, 1), 0.0)
            before = before + jnp.where(lane8 >= 96, pltpu.roll(run[-1], 96, 1), 0.0)
            out.append([r + before for r in run])
        return out

    row8 = lax.broadcasted_iota(jnp.int32, (8, LANES), 0)

    def make_gains(f, _):
        start = f * BINS
        grads, hesss = prefixes(pl.ds(pl.multiple_of(start + BINS - 8, 8), 8))
        for i in range(STEPS):
            s_all = jnp.broadcast_to(hesss[i][7:8], (8, LANES)) + RIDGE
            slope[i] = jnp.broadcast_to(grads[i][7:8], (8, LANES)) / s_all
            total[i] = s_all
            grad_end[pl.ds(i, 1), :] = grads[i][7:8]
            hess_end[pl.ds(i, 1), :] = hesss[i][7:8]

        def chunk(c):
            grads, hesss = prefixes(pl.ds(pl.multiple_of(start + 8 * c, 8), 8))
            split = row8 < jnp.where(c == BINS // 8 - 1, 7, 8)
            out = []
            for i in range(STEPS):
                a = hesss[i]
                apart = grads[i] - a * slope[i]
                product = a * (total[i] - a)
                inverse = pl.reciprocal(product, approx=True)
                inverse = inverse * (2.0 - product * inverse)
                out.append(jnp.where(split, apart * apart * inverse, 0.0))
            return out

        def scan(c, best):
            for k in range(UNROLL):
                best = [jnp.maximum(b, g) for b, g in zip(best, chunk(UNROLL * c + k))]
            return tuple(best)

        best = tuple(jnp.zeros((8, LANES), F32) for _ in range(STEPS))
        best = lax.fori_loop(0, BINS // 8 // UNROLL, scan, best)
        best = jnp.concatenate([jnp.max(b, axis=0, keepdims=True) for b in best], axis=0)
        s_less = hess_end[...]
        g_all = grad_end[...]
        s_all = s_less + RIDGE
        gains[pl.ds(pl.multiple_of(f * STEPS, STEPS), STEPS), :] = s_all * best - g_all * g_all / (s_all * s_less)
        return 0

    lax.fori_loop(0, 2, make_gains, 0)

    for f in range(2):
        rows = gains[pl.ds(f * STEPS, STEPS), :]
        for r in range(QUARTERS):
            rolled[pl.ds(f * 32 + r * STEPS, STEPS), :] = rows if r == 0 else pltpu.roll(rows, 32 * r, 1)
    packed = []
    for f in range(2):
        for a in range(4):
            row = None
            for q in range(4):
                picked = rolled[pl.ds(f * 32 + fold_row[4 * q + a], 1), :]
                row = picked if row is None else jnp.where(lane >= 32 * q, picked, row)
            packed.append(row)
    packed = jnp.concatenate(packed, axis=0)
    send4[...] = packed
    top4[...] = jnp.maximum(packed[:4], packed[4:])

    mine = pl.ds(pl.multiple_of(tm * 8, 8), 8)
    slot = recv_top.at[core * n_tm + tm]
    for d in tm_order:
        send(top4, slot, send_sems.at[4], recv_sems.at[4], tm_other(d))
        if d > 0:
            send(top4, slot, send_sems.at[4], recv_sems.at[4], tm_peer(d))
    pltpu.make_async_copy(top4, slot, recv_sems.at[4]).start()
    for d in tm_order[:-1]:
        send(send4, recv4.at[mine], send_sems.at[3], recv_sems.at[3], tm_peer(d))
    pltpu.make_async_copy(send4, recv4.at[mine], recv_sems.at[3]).start()
    wait(recv_top, recv_sems.at[4])

    send5[...] = largest([recv_top[k] for k in range(2 * n_tm)])
    for d in z_order:
        send(send5, recv5.at[z], send_sems.at[5], recv_sems.at[5], z_peer(d))
    pltpu.make_async_copy(send5, recv5.at[z], recv_sems.at[5]).start()

    wait(recv4, recv_sems.at[3])
    for a in range(4):
        turned = jnp.transpose(recv4[pl.ds(a, 2 * n_tm, stride=4), :])
        for q in range(4):
            split_ref[4 * q + a] = turned[32 * q : 32 * q + 32]

    wait(recv0.at[pl.ds(0, n_tm - 1)], send_sems.at[0])
    wait(recv1.at[pl.ds(0, 2 * n_tm - 1)], send_sems.at[1])
    wait(recv2.at[pl.ds(0, n_z - 1)], send_sems.at[2])
    wait(recv4.at[pl.ds(0, 8 * (n_tm - 1))], send_sems.at[3])
    wait(recv_top.at[pl.ds(0, 2 * n_tm - 1)], send_sems.at[4])
    wait(recv5, recv_sems.at[5])
    planes_ref[...] = recv5[...]
    wait(recv5.at[pl.ds(0, n_z - 1)], send_sems.at[5])


def local(n_tm, n_feat, bin_index, node_ids, logits, labels, roots):
    n_z = n_feat // 2
    bins = bin_index.reshape(4, 8, 8, LANES).transpose(0, 2, 1, 3).reshape(256, LANES)
    operands = (bins, node_ids.reshape(8, LANES), logits.reshape(1, 32), labels.reshape(1, 32), roots)
    vmem = pl.BlockSpec(memory_space=pltpu.VMEM)
    hbm = pl.BlockSpec(memory_space=pltpu.HBM)
    split, planes = pl.pallas_call(
        functools.partial(kernel, n_tm, n_z),
        out_shape=(
            jax.ShapeDtypeStruct((FOLDS, NODES, 2 * n_tm), F32),
            jax.ShapeDtypeStruct((n_z, 4, LANES), F32),
        ),
        in_specs=[hbm] * 5,
        out_specs=(vmem, vmem),
        scratch_shapes=[
            pltpu.VMEM((256, LANES), jnp.int32),
            pltpu.VMEM((8, LANES), jnp.int32),
            pltpu.VMEM((1, 32), F32),
            pltpu.VMEM((1, 32), jnp.int32),
            pltpu.SMEM((FOLDS,), jnp.int32),
            pltpu.SMEM((FOLDS,), jnp.int32),
            pltpu.VMEM((n_tm, 32, LANES), BF16),
            pltpu.VMEM((n_tm, 32, LANES), BF16),
            pltpu.VMEM((1, LANES), F32),
            pltpu.VMEM((2 * n_tm, 1, LANES), F32),
            pltpu.VMEM((n_tm, LANES), BF16),
            pltpu.VMEM((n_z, n_tm, LANES), BF16),
            pltpu.VMEM((8, LANES), F32),
            pltpu.VMEM((8 * n_tm, LANES), F32),
            pltpu.VMEM((4, LANES), F32),
            pltpu.VMEM((2 * n_tm, 4, LANES), F32),
            pltpu.VMEM((4, LANES), F32),
            pltpu.VMEM((n_z, 4, LANES), F32),
            pltpu.VMEM((SUBS, 4, 2 * BINS, QUARTERS * LANES), BF16),
            pltpu.VMEM((SUBS, 4, QUARTERS, LANES), F32),
            pltpu.VMEM((STEPS, 2 * BINS, 2 * LANES), F32),
            pltpu.VMEM((STEPS, 8, LANES), F32),
            pltpu.VMEM((STEPS, 8, LANES), F32),
            pltpu.VMEM((STEPS, LANES), F32),
            pltpu.VMEM((STEPS, LANES), F32),
            pltpu.VMEM((2 * STEPS, LANES), F32),
            pltpu.VMEM((2 * QUARTERS * STEPS, LANES), F32),
            pltpu.SemaphoreType.DMA((5,)),
            pltpu.SemaphoreType.DMA((6,)),
            pltpu.SemaphoreType.DMA((6,)),
            pltpu.SemaphoreType.DMA((SUBS,)),
            pltpu.SemaphoreType.REGULAR,
        ],
        compiler_params=pltpu.CompilerParams(
            collective_id=0, has_side_effects=True, vmem_limit_bytes=32 * 1024 * 1024
        ),
    )(*[pltpu.with_memory_space_constraint(x, pltpu.HBM) for x in operands])
    return pl.pallas_call(
        finish,
        out_shape=(
            jax.ShapeDtypeStruct((FOLDS, NODES, 2 * n_tm), F32),
            jax.ShapeDtypeStruct((FOLDS, NODES), F32),
        ),
        in_specs=[vmem, vmem],
        out_specs=(hbm, hbm),
        scratch_shapes=[pltpu.VMEM((FOLDS, NODES), F32), pltpu.SemaphoreType.DMA((2,))],
        compiler_params=pltpu.CompilerParams(vmem_limit_bytes=4 * 1024 * 1024),
    )(split, planes)


def solution(mesh):
    in_specs = (P("feat", "tm"), P("tm"), P(("tm", "feat")), P(("tm", "feat")), P())
    out_specs = (P(None, None, "feat"), P())
    body = functools.partial(local, mesh.shape["tm"], mesh.shape["feat"])
    return jax.shard_map(body, mesh=mesh, in_specs=in_specs, out_specs=out_specs, check_vma=False)
```

```python
import functools

import jax
import jax.numpy as jnp
from jax import lax
from jax.experimental import pallas as pl
from jax.experimental.pallas import tpu as pltpu
from jax.sharding import PartitionSpec as P

BINS = 256
NODES = 32
FOLDS = 16
LANES = 128
STEPS = 8
QUARTERS = 4
SUBS = 8
MESH = pl.DeviceIdType.MESH
RIDGE = 1.0
PAIR_ORDER = (
    (0, 1, 2, 3, 7, 6, 5, 4),
    (1, 0, 2, 3, 7, 6, 4, 5),
    (2, 1, 3, 0, 4, 7, 5, 6),
    (3, 2, 1, 0, 4, 5, 6, 7),
    (4, 3, 5, 2, 6, 1, 0, 7),
    (5, 4, 6, 3, 7, 2, 0, 1),
    (6, 7, 5, 0, 4, 1, 3, 2),
    (7, 0, 6, 1, 5, 2, 3, 4),
)
UNROLL = 32
F32 = jnp.float32
BF16 = jnp.bfloat16


def largest(rows):
    while len(rows) > 1:
        rest = rows[len(rows) // 2 * 2 :]
        rows = [jnp.maximum(a, b) for a, b in zip(rows[::2], rows[1::2])] + rest
    return rows[0]


def finish(split_ref, planes_ref, split_out, best_out, best_ref, sems):
    copy = pltpu.make_async_copy(split_ref, split_out, sems.at[0])
    copy.start()
    top = largest([planes_ref[k] for k in range(planes_ref.shape[0])])
    for q in range(4):
        best_ref[pl.ds(4 * q, 4), :] = top[:, 32 * q : 32 * q + 32]
    best_copy = pltpu.make_async_copy(best_ref, best_out, sems.at[1])
    best_copy.start()
    copy.wait()
    best_copy.wait()


def kernel(
    n_tm,
    n_z,
    bins_hbm,
    node_hbm,
    logits_hbm,
    labels_hbm,
    roots_hbm,
    split_ref,
    planes_ref,
    bins_ref,
    node_ref,
    logits_ref,
    labels_ref,
    roots_ref,
    fold_row,
    send0,
    recv0,
    send1,
    recv1,
    send2,
    recv2,
    send4,
    recv4,
    top4,
    recv_top,
    send5,
    recv5,
    mask,
    node_rows,
    sums,
    slope,
    total,
    grad_end,
    hess_end,
    gains,
    rolled,
    load_sems,
    send_sems,
    recv_sems,
    pair_sems,
    reach,
):
    tm = lax.axis_index("tm")
    feat = lax.axis_index("feat")
    z = feat // 2
    core = lax.rem(feat, 2)

    def tm_peer(d):
        return (lax.rem(tm + d, n_tm), feat)

    def tm_other(d):
        return (lax.rem(tm + d, n_tm), feat + 1 - 2 * core)

    def z_peer(d):
        return (tm, 2 * lax.rem(z + d, n_z) + core)

    def away(d):
        return min(d // 4, 4 - d // 4) + min(d % 4, 4 - d % 4)

    tm_order = sorted(range(n_tm), key=lambda d: -away(d))
    z_order = sorted(range(1, n_z), key=lambda d: -min(d, n_z - d))
    near = n_z // 4
    peers = [tm_other(d) for d in tm_order] + [tm_peer(d) for d in tm_order[:-1]]
    peers += [z_peer(d) for d in z_order if min(d, n_z - d) <= near]

    barrier = pltpu.get_barrier_semaphore()
    for peer in peers:
        pl.semaphore_signal(barrier, inc=1, device_id=peer, device_id_type=MESH)

    loads = [
        pltpu.make_async_copy(src, dst, load_sems.at[k])
        for k, (src, dst) in enumerate(
            [
                (logits_hbm, logits_ref),
                (labels_hbm, labels_ref),
                (bins_hbm, bins_ref),
                (node_hbm, node_ref),
                (roots_hbm, roots_ref),
            ]
        )
    ]
    for load in loads:
        load.start()

    loads[0].wait()
    loads[1].wait()
    logits = jnp.concatenate([logits_ref[...]] * 4, axis=1)
    labels = jnp.concatenate([labels_ref[...]] * 4, axis=1).astype(F32)
    lane = lax.broadcasted_iota(jnp.int32, (1, LANES), 1)
    place = core + 2 * lax.rem(z, 2)
    prob = 1.0 / (1.0 + jnp.exp(-logits))
    send1[...] = jnp.where(lane // 32 == place, prob - labels, 0.0) + jnp.where(
        lane // 32 == lax.rem(place + 2, 4), prob * (1.0 - prob), 0.0
    )

    loads[2].wait()
    loads[3].wait()
    nodes = node_ref[...].astype(F32)
    for t in range(n_tm):
        rows = []
        for f in (2 * t, 2 * t + 1):
            at = (f // 8) * 64 + f % 8
            rows.append(bins_ref[pl.ds(at, 8, stride=8), :].astype(F32))
        send0[t] = jnp.concatenate(rows + [nodes, nodes], axis=0).astype(BF16)

    pl.semaphore_wait(barrier, len(peers))
    pl.semaphore_signal(reach, inc=1, device_id=z_peer(near), device_id_type=MESH)
    pl.semaphore_signal(reach, inc=1, device_id=z_peer(n_z - near), device_id_type=MESH)

    def send(src, dst, send_sem, recv_sem, device):
        pltpu.make_async_remote_copy(
            src_ref=src,
            dst_ref=dst,
            send_sem=send_sem,
            recv_sem=recv_sem,
            device_id=device,
            device_id_type=MESH,
        ).start()

    def wait(whole, sem):
        pltpu.make_async_copy(whole, whole, sem).wait()

    row = recv1.at[core * n_tm + tm]
    for d in tm_order:
        send(send1, row, send_sems.at[1], recv_sems.at[1], tm_other(d))
        if d > 0:
            send(send1, row, send_sems.at[1], recv_sems.at[1], tm_peer(d))
    pltpu.make_async_copy(send1, row, recv_sems.at[1]).start()
    for d in tm_order[:-1]:
        device = tm_peer(d)
        send(send0.at[device[0]], recv0.at[tm], send_sems.at[0], recv_sems.at[0], device)
    pltpu.make_async_copy(send0.at[tm], recv0.at[tm], recv_sems.at[0]).start()

    def clear(i, _):
        sums[i] = jnp.zeros((2 * BINS, 2 * LANES), F32)
        return 0

    lax.fori_loop(0, STEPS, clear, 0)

    loads[4].wait()
    for o in range(FOLDS):
        block = roots_ref[o] - 1
        fold_row[o] = (((o // 4 - (block >> 3)) & 3) << 3) + (block & 7)

    wait(recv1, recv_sems.at[1])
    send2[...] = jnp.concatenate([recv1[t] + recv1[n_tm + t] for t in range(n_tm)], axis=0).astype(BF16)

    pl.semaphore_wait(reach, 2)
    for d in z_order[::-1]:
        send(send2, recv2.at[z], send_sems.at[2], pair_sems.at[z // 2], z_peer(d))
    pltpu.make_async_copy(send2, recv2.at[z], pair_sems.at[z // 2]).start()

    wait(recv0, recv_sems.at[0])
    level = lax.broadcasted_iota(jnp.int32, (16, LANES), 0).astype(F32)
    one = jnp.ones((16, LANES), BF16)
    zero = jnp.zeros((16, LANES), BF16)

    def make_mask(t, _):
        j, tt = t // 4, lax.rem(t, 4)
        tile = recv0[t].astype(F32)
        at = pl.multiple_of(j * LANES, LANES)
        for s in range(SUBS):
            node_rows[s, tt, pl.ds(j, 1), :] = tile[16 + s : 17 + s]
            for f in range(2):
                b16 = jnp.broadcast_to(tile[8 * f + s : 8 * f + s + 1], (16, LANES)).astype(BF16)
                for v in range(BINS // 16):
                    cut = (level + 16.0 * v).astype(BF16)
                    mask[s, tt, pl.ds(f * BINS + 16 * v, 16), pl.ds(at, LANES)] = jnp.where(cut >= b16, one, zero)
        return 0

    lax.fori_loop(0, n_tm, make_mask, 0)

    node_level = lax.broadcasted_iota(jnp.int32, (NODES, LANES), 0).astype(F32)
    low = lax.broadcasted_iota(jnp.int32, (16, LANES), 1) < 64
    blank = jnp.zeros((NODES, LANES), BF16)

    order = 0
    for pair_at, row in enumerate(PAIR_ORDER):
        code = sum(p << 3 * o for o, p in enumerate(row))
        order = jnp.where(z // 2 == pair_at, code, order)

    def pair(o):
        s = (order >> 3 * o) & 7
        wait(recv2.at[pl.ds(2 * s, 2)], pair_sems.at[s])
        return s

    def accumulate(s):
        first = recv2[2 * s].astype(F32)
        second = recv2[2 * s + 1].astype(F32)
        grads = jnp.where(low, first, second)
        hesss = pltpu.roll(jnp.where(low, second, first), 64, 1)
        for tt in range(4):
            node = node_rows[s, tt]
            quarters = []
            for j in range(QUARTERS):
                t = 4 * j + tt
                here = jnp.broadcast_to(node[j : j + 1], (NODES, LANES)) == node_level
                pieces = []
                for kind in (grads, hesss):
                    chosen = jnp.where(here, jnp.broadcast_to(kind[t : t + 1], (NODES, LANES)), 0.0).astype(BF16)
                    pieces += [chosen if q == j else blank for q in range(QUARTERS)]
                quarters.append(jnp.concatenate(pieces, axis=0))
            weights = jnp.concatenate(quarters, axis=1)
            sums[2 * tt + s // 4] += lax.dot_general(
                mask[s, tt], weights, (((1,), (1,)), ((), ())), preferred_element_type=F32
            )

    def accumulate_two(o, _):
        left, right = pair(2 * o), pair(2 * o + 1)
        accumulate(left)
        accumulate(right)
        return 0

    lax.fori_loop(0, SUBS // 2, accumulate_two, 0)

    lane8 = lax.broadcasted_iota(jnp.int32, (8, LANES), 1)
    kinds = (pl.ds(0, LANES), pl.ds(LANES, LANES))

    def prefixes(at):
        out = []
        for cols, ridge in zip(kinds, (0.0, RIDGE)):
            run = [sums[0, at, cols]]
            for i in range(1, STEPS):
                run.append(run[-1] + sums[i, at, cols])
            before = jnp.where(lane8 >= 32, pltpu.roll(run[-1], 32, 1), 0.0) + ridge
            before = before + jnp.where(lane8 >= 64, pltpu.roll(run[-1], 64, 1), 0.0)
            before = before + jnp.where(lane8 >= 96, pltpu.roll(run[-1], 96, 1), 0.0)
            out.append([r + before for r in run])
        return out

    row8 = lax.broadcasted_iota(jnp.int32, (8, LANES), 0)

    def make_gains(f, _):
        start = f * BINS
        grads, hesss = prefixes(pl.ds(pl.multiple_of(start + BINS - 8, 8), 8))
        for i in range(STEPS):
            s_all = jnp.broadcast_to(hesss[i][7:8], (8, LANES)) + RIDGE
            slope[i] = jnp.broadcast_to(grads[i][7:8], (8, LANES)) / s_all
            total[i] = s_all
            grad_end[pl.ds(i, 1), :] = grads[i][7:8]
            hess_end[pl.ds(i, 1), :] = hesss[i][7:8]

        def chunk(c):
            grads, hesss = prefixes(pl.ds(pl.multiple_of(start + 8 * c, 8), 8))
            split = row8 < jnp.where(c == BINS // 8 - 1, 7, 8)
            out = []
            for i in range(STEPS):
                a = hesss[i]
                apart = grads[i] - a * slope[i]
                product = a * (total[i] - a)
                inverse = pl.reciprocal(product, approx=True)
                inverse = inverse * (2.0 - product * inverse)
                out.append(jnp.where(split, apart * apart * inverse, 0.0))
            return out

        def scan(c, best):
            for k in range(UNROLL):
                best = [jnp.maximum(b, g) for b, g in zip(best, chunk(UNROLL * c + k))]
            return tuple(best)

        best = tuple(jnp.zeros((8, LANES), F32) for _ in range(STEPS))
        best = lax.fori_loop(0, BINS // 8 // UNROLL, scan, best)
        best = jnp.concatenate([jnp.max(b, axis=0, keepdims=True) for b in best], axis=0)
        s_less = hess_end[...]
        g_all = grad_end[...]
        s_all = s_less + RIDGE
        gains[pl.ds(pl.multiple_of(f * STEPS, STEPS), STEPS), :] = s_all * best - g_all * g_all / (s_all * s_less)
        return 0

    lax.fori_loop(0, 2, make_gains, 0)

    def fold_rows(k, rows):
        for r in range(QUARTERS):
            rolled[pl.ds(k * 32 + r * STEPS, STEPS), :] = rows if r == 0 else pltpu.roll(rows, 32 * r, 1)
        packed = []
        for a in range(4):
            row = rolled[pl.ds(k * 32 + fold_row[a], 1), :]
            for q in range(1, 4):
                row = jnp.where(lane >= 32 * q, rolled[pl.ds(k * 32 + fold_row[4 * q + a], 1), :], row)
            packed.append(row)
        return jnp.concatenate(packed, axis=0)

    first, second = gains[pl.ds(0, STEPS), :], gains[pl.ds(STEPS, STEPS), :]
    top4[...] = fold_rows(2, jnp.maximum(first, second))
    slot = recv_top.at[core * n_tm + tm]
    for d in tm_order:
        send(top4, slot, send_sems.at[4], recv_sems.at[4], tm_other(d))
        if d > 0:
            send(top4, slot, send_sems.at[4], recv_sems.at[4], tm_peer(d))
    pltpu.make_async_copy(top4, slot, recv_sems.at[4]).start()
    send4[pl.ds(0, 4), :] = fold_rows(0, first)
    send4[pl.ds(4, 4), :] = fold_rows(1, second)
    mine = pl.ds(pl.multiple_of(tm * 8, 8), 8)
    for d in tm_order[:-1]:
        send(send4, recv4.at[mine], send_sems.at[3], recv_sems.at[3], tm_peer(d))
    pltpu.make_async_copy(send4, recv4.at[mine], recv_sems.at[3]).start()
    wait(recv_top, recv_sems.at[4])

    send5[...] = largest([recv_top[k] for k in range(2 * n_tm)])
    for d in z_order:
        send(send5, recv5.at[z], send_sems.at[5], recv_sems.at[5], z_peer(d))
    pltpu.make_async_copy(send5, recv5.at[z], recv_sems.at[5]).start()

    wait(recv4, recv_sems.at[3])
    for a in range(4):
        turned = jnp.transpose(recv4[pl.ds(a, 2 * n_tm, stride=4), :])
        for q in range(4):
            split_ref[4 * q + a] = turned[32 * q : 32 * q + 32]

    wait(recv0.at[pl.ds(0, n_tm - 1)], send_sems.at[0])
    wait(recv1.at[pl.ds(0, 2 * n_tm - 1)], send_sems.at[1])
    wait(recv2.at[pl.ds(0, n_z - 1)], send_sems.at[2])
    wait(recv4.at[pl.ds(0, 8 * (n_tm - 1))], send_sems.at[3])
    wait(recv_top.at[pl.ds(0, 2 * n_tm - 1)], send_sems.at[4])
    wait(recv5, recv_sems.at[5])
    planes_ref[...] = recv5[...]
    wait(recv5.at[pl.ds(0, n_z - 1)], send_sems.at[5])


def local(n_tm, n_feat, bin_index, node_ids, logits, labels, roots):
    n_z = n_feat // 2
    bins = bin_index.reshape(4, 8, 8, LANES).transpose(0, 2, 1, 3).reshape(256, LANES)
    operands = (bins, node_ids.reshape(8, LANES), logits.reshape(1, 32), labels.reshape(1, 32), roots)
    vmem = pl.BlockSpec(memory_space=pltpu.VMEM)
    hbm = pl.BlockSpec(memory_space=pltpu.HBM)
    split, planes = pl.pallas_call(
        functools.partial(kernel, n_tm, n_z),
        out_shape=(
            jax.ShapeDtypeStruct((FOLDS, NODES, 2 * n_tm), F32),
            jax.ShapeDtypeStruct((n_z, 4, LANES), F32),
        ),
        in_specs=[hbm] * 5,
        out_specs=(vmem, vmem),
        scratch_shapes=[
            pltpu.VMEM((256, LANES), jnp.int32),
            pltpu.VMEM((8, LANES), jnp.int32),
            pltpu.VMEM((1, 32), F32),
            pltpu.VMEM((1, 32), jnp.int32),
            pltpu.SMEM((FOLDS,), jnp.int32),
            pltpu.SMEM((FOLDS,), jnp.int32),
            pltpu.VMEM((n_tm, 32, LANES), BF16),
            pltpu.VMEM((n_tm, 32, LANES), BF16),
            pltpu.VMEM((1, LANES), F32),
            pltpu.VMEM((2 * n_tm, 1, LANES), F32),
            pltpu.VMEM((n_tm, LANES), BF16),
            pltpu.VMEM((n_z, n_tm, LANES), BF16),
            pltpu.VMEM((8, LANES), F32),
            pltpu.VMEM((8 * n_tm, LANES), F32),
            pltpu.VMEM((4, LANES), F32),
            pltpu.VMEM((2 * n_tm, 4, LANES), F32),
            pltpu.VMEM((4, LANES), F32),
            pltpu.VMEM((n_z, 4, LANES), F32),
            pltpu.VMEM((SUBS, 4, 2 * BINS, QUARTERS * LANES), BF16),
            pltpu.VMEM((SUBS, 4, QUARTERS, LANES), F32),
            pltpu.VMEM((STEPS, 2 * BINS, 2 * LANES), F32),
            pltpu.VMEM((STEPS, 8, LANES), F32),
            pltpu.VMEM((STEPS, 8, LANES), F32),
            pltpu.VMEM((STEPS, LANES), F32),
            pltpu.VMEM((STEPS, LANES), F32),
            pltpu.VMEM((2 * STEPS, LANES), F32),
            pltpu.VMEM((3 * QUARTERS * STEPS, LANES), F32),
            pltpu.SemaphoreType.DMA((5,)),
            pltpu.SemaphoreType.DMA((6,)),
            pltpu.SemaphoreType.DMA((6,)),
            pltpu.SemaphoreType.DMA((SUBS,)),
            pltpu.SemaphoreType.REGULAR,
        ],
        compiler_params=pltpu.CompilerParams(
            collective_id=0, has_side_effects=True, vmem_limit_bytes=32 * 1024 * 1024
        ),
    )(*[pltpu.with_memory_space_constraint(x, pltpu.HBM) for x in operands])
    return pl.pallas_call(
        finish,
        out_shape=(
            jax.ShapeDtypeStruct((FOLDS, NODES, 2 * n_tm), F32),
            jax.ShapeDtypeStruct((FOLDS, NODES), F32),
        ),
        in_specs=[vmem, vmem],
        out_specs=(hbm, hbm),
        scratch_shapes=[pltpu.VMEM((FOLDS, NODES), F32), pltpu.SemaphoreType.DMA((2,))],
        compiler_params=pltpu.CompilerParams(vmem_limit_bytes=4 * 1024 * 1024),
    )(split, planes)


def solution(mesh):
    in_specs = (P("feat", "tm"), P("tm"), P(("tm", "feat")), P(("tm", "feat")), P())
    out_specs = (P(None, None, "feat"), P())
    body = functools.partial(local, mesh.shape["tm"], mesh.shape["feat"])
    return jax.shard_map(body, mesh=mesh, in_specs=in_specs, out_specs=out_specs, check_vma=False)
```

```python
import functools

import jax
import jax.numpy as jnp
from jax import lax
from jax.experimental import pallas as pl
from jax.experimental.pallas import tpu as pltpu
from jax.sharding import PartitionSpec as P

BINS = 256
NODES = 32
FOLDS = 16
LANES = 128
STEPS = 8
QUARTERS = 4
SUBS = 8
MESH = pl.DeviceIdType.MESH
RIDGE = 1.0
PAIR_ORDER = (
    (0, 1, 2, 3, 7, 6, 5, 4),
    (1, 0, 2, 3, 7, 6, 4, 5),
    (2, 1, 3, 0, 4, 7, 5, 6),
    (3, 2, 1, 0, 4, 5, 6, 7),
    (4, 3, 5, 2, 6, 1, 0, 7),
    (5, 4, 6, 3, 7, 2, 0, 1),
    (6, 7, 5, 0, 4, 1, 3, 2),
    (7, 0, 6, 1, 5, 2, 3, 4),
)
UNROLL = 32
F32 = jnp.float32
BF16 = jnp.bfloat16


def largest(rows):
    while len(rows) > 1:
        rest = rows[len(rows) // 2 * 2 :]
        rows = [jnp.maximum(a, b) for a, b in zip(rows[::2], rows[1::2])] + rest
    return rows[0]


def finish(split_ref, planes_ref, split_out, best_out, best_ref, sems):
    copy = pltpu.make_async_copy(split_ref, split_out, sems.at[0])
    copy.start()
    top = largest([planes_ref[k] for k in range(planes_ref.shape[0])])
    for q in range(4):
        best_ref[pl.ds(4 * q, 4), :] = top[:, 32 * q : 32 * q + 32]
    best_copy = pltpu.make_async_copy(best_ref, best_out, sems.at[1])
    best_copy.start()
    copy.wait()
    best_copy.wait()


def kernel(
    n_tm,
    n_z,
    bins_hbm,
    node_hbm,
    logits_hbm,
    labels_hbm,
    roots_hbm,
    split_ref,
    planes_ref,
    bins_ref,
    node_ref,
    logits_ref,
    labels_ref,
    roots_ref,
    fold_row,
    send0,
    recv0,
    send1,
    recv1,
    send2,
    recv2,
    send4,
    recv4,
    top4,
    recv_top,
    send5,
    recv5,
    rows32,
    cuts,
    sums,
    slope,
    total,
    grad_end,
    hess_end,
    gains,
    rolled,
    load_sems,
    send_sems,
    recv_sems,
    pair_sems,
    reach,
):
    tm = lax.axis_index("tm")
    feat = lax.axis_index("feat")
    z = feat // 2
    core = lax.rem(feat, 2)

    def tm_peer(d):
        return (lax.rem(tm + d, n_tm), feat)

    def tm_other(d):
        return (lax.rem(tm + d, n_tm), feat + 1 - 2 * core)

    def z_peer(d):
        return (tm, 2 * lax.rem(z + d, n_z) + core)

    def away(d):
        return min(d // 4, 4 - d // 4) + min(d % 4, 4 - d % 4)

    tm_order = sorted(range(n_tm), key=lambda d: -away(d))
    z_order = sorted(range(1, n_z), key=lambda d: -min(d, n_z - d))
    near = n_z // 4
    peers = [tm_other(d) for d in tm_order] + [tm_peer(d) for d in tm_order[:-1]]
    peers += [z_peer(d) for d in z_order if min(d, n_z - d) <= near]

    barrier = pltpu.get_barrier_semaphore()
    for peer in peers:
        pl.semaphore_signal(barrier, inc=1, device_id=peer, device_id_type=MESH)

    loads = [
        pltpu.make_async_copy(src, dst, load_sems.at[k])
        for k, (src, dst) in enumerate(
            [
                (logits_hbm, logits_ref),
                (labels_hbm, labels_ref),
                (bins_hbm, bins_ref),
                (node_hbm, node_ref),
                (roots_hbm, roots_ref),
            ]
        )
    ]
    for load in loads:
        load.start()

    loads[0].wait()
    loads[1].wait()
    logits = jnp.concatenate([logits_ref[...]] * 4, axis=1)
    labels = jnp.concatenate([labels_ref[...]] * 4, axis=1).astype(F32)
    lane = lax.broadcasted_iota(jnp.int32, (1, LANES), 1)
    place = core + 2 * lax.rem(z, 2)
    prob = 1.0 / (1.0 + jnp.exp(-logits))
    send1[...] = jnp.where(lane // 32 == place, prob - labels, 0.0) + jnp.where(
        lane // 32 == lax.rem(place + 2, 4), prob * (1.0 - prob), 0.0
    )

    loads[2].wait()
    loads[3].wait()
    nodes = node_ref[...].astype(F32)
    for t in range(n_tm):
        rows = []
        for f in (2 * t, 2 * t + 1):
            at = (f // 8) * 64 + f % 8
            rows.append(bins_ref[pl.ds(at, 8, stride=8), :].astype(F32))
        send0[t] = jnp.concatenate(rows + [nodes, nodes], axis=0).astype(BF16)

    pl.semaphore_wait(barrier, len(peers))
    pl.semaphore_signal(reach, inc=1, device_id=z_peer(near), device_id_type=MESH)
    pl.semaphore_signal(reach, inc=1, device_id=z_peer(n_z - near), device_id_type=MESH)

    def send(src, dst, send_sem, recv_sem, device):
        pltpu.make_async_remote_copy(
            src_ref=src,
            dst_ref=dst,
            send_sem=send_sem,
            recv_sem=recv_sem,
            device_id=device,
            device_id_type=MESH,
        ).start()

    def wait(whole, sem):
        pltpu.make_async_copy(whole, whole, sem).wait()

    row = recv1.at[core * n_tm + tm]
    for d in tm_order:
        send(send1, row, send_sems.at[1], recv_sems.at[1], tm_other(d))
        if d > 0:
            send(send1, row, send_sems.at[1], recv_sems.at[1], tm_peer(d))
    pltpu.make_async_copy(send1, row, recv_sems.at[1]).start()
    for d in tm_order[:-1]:
        device = tm_peer(d)
        send(send0.at[device[0]], recv0.at[tm], send_sems.at[0], recv_sems.at[0], device)
    pltpu.make_async_copy(send0.at[tm], recv0.at[tm], recv_sems.at[0]).start()

    def clear(i, _):
        sums[i] = jnp.zeros((2 * BINS, 2 * LANES), F32)
        return 0

    lax.fori_loop(0, STEPS, clear, 0)

    loads[4].wait()
    for o in range(FOLDS):
        block = roots_ref[o] - 1
        fold_row[o] = (((o // 4 - (block >> 3)) & 3) << 3) + (block & 7)

    cuts[...] = lax.broadcasted_iota(jnp.int32, (BINS, LANES), 0).astype(F32).astype(BF16)
    wait(recv1, recv_sems.at[1])
    send2[...] = jnp.concatenate([recv1[t] + recv1[n_tm + t] for t in range(n_tm)], axis=0).astype(BF16)

    pl.semaphore_wait(reach, 2)
    for d in z_order[::-1]:
        send(send2, recv2.at[z], send_sems.at[2], pair_sems.at[z // 2], z_peer(d))
    pltpu.make_async_copy(send2, recv2.at[z], pair_sems.at[z // 2]).start()

    wait(recv0, recv_sems.at[0])
    for t in range(n_tm):
        rows32[t] = recv0[t].astype(F32)[:24]
    one = jnp.ones((16, LANES), BF16)
    zero = jnp.zeros((16, LANES), BF16)

    def mask(s, tt):
        columns = []
        for j in range(QUARTERS):
            tiles = []
            for f in range(2):
                row = rows32[4 * j + tt, pl.ds(8 * f + s, 1), :]
                b16 = jnp.broadcast_to(row, (16, LANES)).astype(BF16)
                for v in range(BINS // 16):
                    tiles.append(jnp.where(cuts[pl.ds(16 * v, 16), :] >= b16, one, zero))
            columns.append(jnp.concatenate(tiles, axis=0))
        return jnp.concatenate(columns, axis=1)

    node_level = lax.broadcasted_iota(jnp.int32, (NODES, LANES), 0).astype(F32)
    low = lax.broadcasted_iota(jnp.int32, (16, LANES), 1) < 64
    blank = jnp.zeros((NODES, LANES), BF16)

    order = 0
    for pair_at, row in enumerate(PAIR_ORDER):
        code = sum(p << 3 * o for o, p in enumerate(row))
        order = jnp.where(z // 2 == pair_at, code, order)

    def pair(o):
        s = (order >> 3 * o) & 7
        wait(recv2.at[pl.ds(2 * s, 2)], pair_sems.at[s])
        return s

    def accumulate(s):
        first = recv2[2 * s].astype(F32)
        second = recv2[2 * s + 1].astype(F32)
        grads = jnp.where(low, first, second)
        hesss = pltpu.roll(jnp.where(low, second, first), 64, 1)
        for tt in range(4):
            quarters = []
            for j in range(QUARTERS):
                t = 4 * j + tt
                here = jnp.broadcast_to(rows32[t, pl.ds(16 + s, 1), :], (NODES, LANES)) == node_level
                pieces = []
                for kind in (grads, hesss):
                    chosen = jnp.where(here, jnp.broadcast_to(kind[t : t + 1], (NODES, LANES)), 0.0).astype(BF16)
                    pieces += [chosen if q == j else blank for q in range(QUARTERS)]
                quarters.append(jnp.concatenate(pieces, axis=0))
            weights = jnp.concatenate(quarters, axis=1)
            sums[2 * tt + s // 4] += lax.dot_general(
                mask(s, tt), weights, (((1,), (1,)), ((), ())), preferred_element_type=F32
            )

    def accumulate_two(o, _):
        left, right = pair(2 * o), pair(2 * o + 1)
        accumulate(left)
        accumulate(right)
        return 0

    lax.fori_loop(0, SUBS // 2, accumulate_two, 0)

    lane8 = lax.broadcasted_iota(jnp.int32, (8, LANES), 1)
    kinds = (pl.ds(0, LANES), pl.ds(LANES, LANES))

    def prefixes(at):
        out = []
        for cols, ridge in zip(kinds, (0.0, RIDGE)):
            run = [sums[0, at, cols]]
            for i in range(1, STEPS):
                run.append(run[-1] + sums[i, at, cols])
            before = jnp.where(lane8 >= 32, pltpu.roll(run[-1], 32, 1), 0.0) + ridge
            before = before + jnp.where(lane8 >= 64, pltpu.roll(run[-1], 64, 1), 0.0)
            before = before + jnp.where(lane8 >= 96, pltpu.roll(run[-1], 96, 1), 0.0)
            out.append([r + before for r in run])
        return out

    row8 = lax.broadcasted_iota(jnp.int32, (8, LANES), 0)

    def make_gains(f, _):
        start = f * BINS
        grads, hesss = prefixes(pl.ds(pl.multiple_of(start + BINS - 8, 8), 8))
        for i in range(STEPS):
            s_all = jnp.broadcast_to(hesss[i][7:8], (8, LANES)) + RIDGE
            slope[i] = jnp.broadcast_to(grads[i][7:8], (8, LANES)) / s_all
            total[i] = s_all
            grad_end[pl.ds(i, 1), :] = grads[i][7:8]
            hess_end[pl.ds(i, 1), :] = hesss[i][7:8]

        def chunk(c):
            grads, hesss = prefixes(pl.ds(pl.multiple_of(start + 8 * c, 8), 8))
            split = row8 < jnp.where(c == BINS // 8 - 1, 7, 8)
            out = []
            for i in range(STEPS):
                a = hesss[i]
                apart = grads[i] - a * slope[i]
                product = a * (total[i] - a)
                inverse = pl.reciprocal(product, approx=True)
                inverse = inverse * (2.0 - product * inverse)
                out.append(jnp.where(split, apart * apart * inverse, 0.0))
            return out

        def scan(c, best):
            for k in range(UNROLL):
                best = [jnp.maximum(b, g) for b, g in zip(best, chunk(UNROLL * c + k))]
            return tuple(best)

        best = tuple(jnp.zeros((8, LANES), F32) for _ in range(STEPS))
        best = lax.fori_loop(0, BINS // 8 // UNROLL, scan, best)
        best = jnp.concatenate([jnp.max(b, axis=0, keepdims=True) for b in best], axis=0)
        s_less = hess_end[...]
        g_all = grad_end[...]
        s_all = s_less + RIDGE
        gains[pl.ds(pl.multiple_of(f * STEPS, STEPS), STEPS), :] = s_all * best - g_all * g_all / (s_all * s_less)
        return 0

    lax.fori_loop(0, 2, make_gains, 0)

    def fold_rows(k, rows):
        for r in range(QUARTERS):
            rolled[pl.ds(k * 32 + r * STEPS, STEPS), :] = rows if r == 0 else pltpu.roll(rows, 32 * r, 1)
        packed = []
        for a in range(4):
            row = rolled[pl.ds(k * 32 + fold_row[a], 1), :]
            for q in range(1, 4):
                row = jnp.where(lane >= 32 * q, rolled[pl.ds(k * 32 + fold_row[4 * q + a], 1), :], row)
            packed.append(row)
        return jnp.concatenate(packed, axis=0)

    first, second = gains[pl.ds(0, STEPS), :], gains[pl.ds(STEPS, STEPS), :]
    top4[...] = fold_rows(2, jnp.maximum(first, second))
    slot = recv_top.at[core * n_tm + tm]
    for d in tm_order:
        send(top4, slot, send_sems.at[4], recv_sems.at[4], tm_other(d))
        if d > 0:
            send(top4, slot, send_sems.at[4], recv_sems.at[4], tm_peer(d))
    pltpu.make_async_copy(top4, slot, recv_sems.at[4]).start()
    send4[pl.ds(0, 4), :] = fold_rows(0, first)
    send4[pl.ds(4, 4), :] = fold_rows(1, second)
    mine = pl.ds(pl.multiple_of(tm * 8, 8), 8)
    for d in tm_order[:-1]:
        send(send4, recv4.at[mine], send_sems.at[3], recv_sems.at[3], tm_peer(d))
    pltpu.make_async_copy(send4, recv4.at[mine], recv_sems.at[3]).start()
    wait(recv_top, recv_sems.at[4])

    send5[...] = largest([recv_top[k] for k in range(2 * n_tm)])
    for d in z_order:
        send(send5, recv5.at[z], send_sems.at[5], recv_sems.at[5], z_peer(d))
    pltpu.make_async_copy(send5, recv5.at[z], recv_sems.at[5]).start()

    wait(recv4, recv_sems.at[3])
    for a in range(4):
        turned = jnp.transpose(recv4[pl.ds(a, 2 * n_tm, stride=4), :])
        for q in range(4):
            split_ref[4 * q + a] = turned[32 * q : 32 * q + 32]

    wait(recv0.at[pl.ds(0, n_tm - 1)], send_sems.at[0])
    wait(recv1.at[pl.ds(0, 2 * n_tm - 1)], send_sems.at[1])
    wait(recv2.at[pl.ds(0, n_z - 1)], send_sems.at[2])
    wait(recv4.at[pl.ds(0, 8 * (n_tm - 1))], send_sems.at[3])
    wait(recv_top.at[pl.ds(0, 2 * n_tm - 1)], send_sems.at[4])
    wait(recv5, recv_sems.at[5])
    planes_ref[...] = recv5[...]
    wait(recv5.at[pl.ds(0, n_z - 1)], send_sems.at[5])


def local(n_tm, n_feat, bin_index, node_ids, logits, labels, roots):
    n_z = n_feat // 2
    bins = bin_index.reshape(4, 8, 8, LANES).transpose(0, 2, 1, 3).reshape(256, LANES)
    operands = (bins, node_ids.reshape(8, LANES), logits.reshape(1, 32), labels.reshape(1, 32), roots)
    vmem = pl.BlockSpec(memory_space=pltpu.VMEM)
    hbm = pl.BlockSpec(memory_space=pltpu.HBM)
    split, planes = pl.pallas_call(
        functools.partial(kernel, n_tm, n_z),
        out_shape=(
            jax.ShapeDtypeStruct((FOLDS, NODES, 2 * n_tm), F32),
            jax.ShapeDtypeStruct((n_z, 4, LANES), F32),
        ),
        in_specs=[hbm] * 5,
        out_specs=(vmem, vmem),
        scratch_shapes=[
            pltpu.VMEM((256, LANES), jnp.int32),
            pltpu.VMEM((8, LANES), jnp.int32),
            pltpu.VMEM((1, 32), F32),
            pltpu.VMEM((1, 32), jnp.int32),
            pltpu.SMEM((FOLDS,), jnp.int32),
            pltpu.SMEM((FOLDS,), jnp.int32),
            pltpu.VMEM((n_tm, 32, LANES), BF16),
            pltpu.VMEM((n_tm, 32, LANES), BF16),
            pltpu.VMEM((1, LANES), F32),
            pltpu.VMEM((2 * n_tm, 1, LANES), F32),
            pltpu.VMEM((n_tm, LANES), BF16),
            pltpu.VMEM((n_z, n_tm, LANES), BF16),
            pltpu.VMEM((8, LANES), F32),
            pltpu.VMEM((8 * n_tm, LANES), F32),
            pltpu.VMEM((4, LANES), F32),
            pltpu.VMEM((2 * n_tm, 4, LANES), F32),
            pltpu.VMEM((4, LANES), F32),
            pltpu.VMEM((n_z, 4, LANES), F32),
            pltpu.VMEM((n_tm, 24, LANES), F32),
            pltpu.VMEM((BINS, LANES), BF16),
            pltpu.VMEM((STEPS, 2 * BINS, 2 * LANES), F32),
            pltpu.VMEM((STEPS, 8, LANES), F32),
            pltpu.VMEM((STEPS, 8, LANES), F32),
            pltpu.VMEM((STEPS, LANES), F32),
            pltpu.VMEM((STEPS, LANES), F32),
            pltpu.VMEM((2 * STEPS, LANES), F32),
            pltpu.VMEM((3 * QUARTERS * STEPS, LANES), F32),
            pltpu.SemaphoreType.DMA((5,)),
            pltpu.SemaphoreType.DMA((6,)),
            pltpu.SemaphoreType.DMA((6,)),
            pltpu.SemaphoreType.DMA((SUBS,)),
            pltpu.SemaphoreType.REGULAR,
        ],
        compiler_params=pltpu.CompilerParams(
            collective_id=0, has_side_effects=True, vmem_limit_bytes=32 * 1024 * 1024
        ),
    )(*[pltpu.with_memory_space_constraint(x, pltpu.HBM) for x in operands])
    return pl.pallas_call(
        finish,
        out_shape=(
            jax.ShapeDtypeStruct((FOLDS, NODES, 2 * n_tm), F32),
            jax.ShapeDtypeStruct((FOLDS, NODES), F32),
        ),
        in_specs=[vmem, vmem],
        out_specs=(hbm, hbm),
        scratch_shapes=[pltpu.VMEM((FOLDS, NODES), F32), pltpu.SemaphoreType.DMA((2,))],
        compiler_params=pltpu.CompilerParams(vmem_limit_bytes=4 * 1024 * 1024),
    )(split, planes)


def solution(mesh):
    in_specs = (P("feat", "tm"), P("tm"), P(("tm", "feat")), P(("tm", "feat")), P())
    out_specs = (P(None, None, "feat"), P())
    body = functools.partial(local, mesh.shape["tm"], mesh.shape["feat"])
    return jax.shard_map(body, mesh=mesh, in_specs=in_specs, out_specs=out_specs, check_vma=False)
```
